512 devices in a mesh: sector: 32 (over x, y), op: 16 (over z, core).
Axes of the slice: x: 4, y: 8, z: 8, core: 2. Of those that a mesh axis runs over, the one named last changes fastest.
Arguments:
- wavefunction: bfloat16 [2, 256, 128, 128], P(None, 'sector'), may hold values from -6 to 6
- right_blocks: bfloat16 [256, 128, 128, 128], P('sector', 'op'), may hold values from -0.5 to 0.5
- left_blocks: bfloat16 [256, 128, 128, 128], P('sector', 'op'), may hold values from -0.0625 to 0.0625
- targets: int32 [256, 128], P('sector', 'op'), may hold values from 0 to 255, as said below
Outputs:
- sigma_blocks: float32 [2, 256, 128, 128], P(None, 'sector', 'op')
The draws below stay inside these ranges and needn't reach their ends.
Inputs may be any that keep to these rules, and one draw needn't show every extreme that they name: Sector t is owned by index t // 8 of sector. Among the pairs of one device (8 source sectors times the 8 terms of one op index) at most 4 have targets on any one owner; in every draw one owner receives exactly 4 from every device.
All inputs are finite; a program needn't handle non-finite values.
Results may differ from the reference program's by a relative error of at most 0.0037.
Values may be sent and summed in bfloat16 or wider, within the bound.
No kernel may reach another device: no remote copies, remote signals or barrier semaphores. Data moves between devices by JAX's collectives and lax.ppermute only.
A program may use at most 64 MiB of HBM per device.

```python
import jax
import jax.numpy as jnp
from jax import lax

M = 128
SEC_DEV = 8
TERM_DEV = 8
NS = 256
KT = 128
CAP = 4


def draw_targets(key, part):
    key = jax.random.fold_in(key, 5)
    group_count = NS // SEC_DEV
    op_count = KT // TERM_DEV
    pair_count = SEC_DEV * TERM_DEV
    slot_count = group_count * CAP
    busiest = jax.random.randint(jax.random.fold_in(key, 1), (), 0, group_count).astype(jnp.int32)

    def one_device(index):
        device_key = jax.random.fold_in(key, index + 7)
        key_one, key_two, key_three = jax.random.split(device_key, 3)
        shuffled = jax.random.permutation(key_one, jnp.arange(slot_count, dtype=jnp.int32))
        owners = shuffled // CAP
        counter = jnp.arange(slot_count, dtype=jnp.int32)
        score = jnp.where(owners == busiest, slot_count + counter, counter)
        order = jnp.argsort(score)
        others = owners[order][:pair_count - CAP]
        chosen = jnp.concatenate([jnp.full((CAP,), busiest, jnp.int32), others.astype(jnp.int32)])
        chosen = jax.random.permutation(key_two, chosen)
        local_ids = jax.random.randint(key_three, (pair_count,), 0, SEC_DEV).astype(jnp.int32)
        return (chosen * SEC_DEV + local_ids).astype(jnp.int32)
    values = jax.vmap(one_device)(jnp.arange(group_count * op_count, dtype=jnp.int32))
    values = values.reshape(group_count, op_count, SEC_DEV, TERM_DEV)
    return jnp.transpose(values, (0, 2, 1, 3)).reshape(NS, KT).astype(jnp.int32)


def strengthened(drawn, own_key, source, target, blocks, factor):
    owner, partner = [(jnp.arange(drawn.shape[position]) // (drawn.shape[position] // blocks)).reshape([-1 if axis == position else 1 for axis in range(drawn.ndim)]) for position in (source, target)]
    chosen = jax.random.permutation(own_key, blocks)[partner]
    strong = (owner == chosen) | (owner == (partner + blocks // 2) % blocks)
    return jnp.where(strong, factor * drawn, drawn)


def block_levels(stream_key, extent, shards, smallest, high):
    def one(position, blocks):
        steps = jax.random.uniform(jax.random.fold_in(jax.random.fold_in(stream_key, 6), position), (blocks,), jnp.float32, smallest / len(shards), high / len(shards))
        return jnp.repeat(jnp.exp(steps), extent[position] // blocks).reshape((-1,) + (1,) * (len(extent) - position - 1))

    factor_of = one(*shards[0])
    for cut in shards[1:]:
        factor_of = factor_of * one(*cut)
    return factor_of


def centred(rng, extent, width, bound, pieces=(), kind=jnp.bfloat16):
    array = jax.random.normal(rng, extent, jnp.float32) * width
    if len(pieces) > 0:
        array = block_levels(rng, extent, pieces, -0.22, 0.18) * array
    return jnp.clip(array, min=-bound, max=bound).astype(kind)


def noise_with(own_key, shape, spread, bound, cuts, heavy, kind=jnp.bfloat16):
    values = spread * jax.random.normal(own_key, shape, jnp.float32)
    if cuts:
        values = values * block_levels(own_key, shape, cuts, -0.22, 0.18)
    return jnp.clip(strengthened(values, jax.random.fold_in(own_key, 3), *heavy), -bound, bound).astype(kind)


def setup_inputs(seed: int = 0) -> dict:
    streams_of = jax.random.split(jax.random.key(seed), 5)
    wavefunction = centred(streams_of[0], (2, NS, M, M), 1.0, 6.0, ((1, 32),))
    right_blocks = centred(streams_of[1], (NS, KT, M, M), M ** -0.5, 0.5, ((0, 32), (1, 16)))
    left_blocks = noise_with(streams_of[2], (NS, KT, M, M), (M * KT) ** -0.5, 0.0625, ((0, 32), (1, 16)), (1, 2, 16, 2.0))
    targets = draw_targets(jax.random.fold_in(streams_of[4], 71), 0)
    return {"wavefunction": wavefunction, "right_blocks": right_blocks, "left_blocks": left_blocks, "targets": targets}


def reference(wavefunction, right_blocks, left_blocks, targets):
    vectors = wavefunction.astype(jnp.float32)
    sector_ids = jnp.arange(NS, dtype=jnp.int32)

    def one_term(sigma_blocks, term):
        right_term = right_blocks[:, term].astype(jnp.float32)
        wave = jnp.einsum("vsab,scb->vsac", vectors, right_term, precision=lax.Precision.HIGHEST).astype(jnp.bfloat16)
        wave = lax.optimization_barrier(wave)
        target_col = targets[:, term]
        onehot = (target_col[:, None] == sector_ids[None, :]).astype(jnp.float32)
        grouped = jnp.einsum("st,vsac->vtac", onehot, wave.astype(jnp.float32), precision=lax.Precision.HIGHEST).astype(jnp.bfloat16)
        grouped = lax.optimization_barrier(grouped)
        left_term = left_blocks[:, term].astype(jnp.float32)
        products = jnp.einsum("tab,vtbc->vtac", left_term, grouped.astype(jnp.float32), precision=lax.Precision.HIGHEST)
        return sigma_blocks + products, None

    initial = jnp.zeros((2, NS, M, M), jnp.float32)
    result, unused = lax.scan(one_term, initial, jnp.arange(KT, dtype=jnp.int32))
    return result
```

```python
import functools

import jax
import jax.numpy as jnp
from jax import lax
from jax.experimental import pallas as pl
from jax.experimental.pallas import tpu as pltpu
from jax.sharding import PartitionSpec as P

X, Y, Z, CORES = 4, 8, 8, 2
CAP = 4


def z_ring():
    return [
        (z * CORES + c, ((z + 1 - 2 * c) % Z) * CORES + c) for z in range(Z) for c in range(CORES)
    ]


def core_swap():
    return [(z * CORES + c, z * CORES + 1 - c) for z in range(Z) for c in range(CORES)]


def x_shift(distance):
    return [(x * Y + y, ((x + distance) % X) * Y + y) for x in range(X) for y in range(Y)]


def pack_kernel(targets_ref, right_ref, packed_ref, counts_ref):
    groups = counts_ref.shape[0]
    sectors, terms = targets_ref.shape

    def clear(g, carry):
        counts_ref[g] = 0
        return carry

    lax.fori_loop(0, groups, clear, 0)

    def place(s, carry):
        for k in range(terms):
            owner = targets_ref[s, k] >> 3
            position = counts_ref[owner]
            counts_ref[owner] = position + 1
            packed_ref[owner * CAP + position] = right_ref[s, k]
        return carry

    lax.fori_loop(0, sectors, place, 0)


def pack(targets, right_blocks, groups):
    _, _, rows, cols = right_blocks.shape
    return pl.pallas_call(
        pack_kernel,
        out_shape=jax.ShapeDtypeStruct((groups * CAP, rows, cols), right_blocks.dtype),
        in_specs=[
            pl.BlockSpec(memory_space=pltpu.SMEM),
            pl.BlockSpec(memory_space=pltpu.VMEM),
        ],
        out_specs=pl.BlockSpec(memory_space=pltpu.VMEM),
        scratch_shapes=[pltpu.SMEM((groups,), jnp.int32)],
        compiler_params=pltpu.CompilerParams(vmem_limit_bytes=16 * 2**20),
        cost_estimate=pl.CostEstimate(flops=0, bytes_accessed=8 * 2**20, transcendentals=0),
        name="pack_blocks",
    )(targets, right_blocks)


UNROLL = 8
GROUP_BITS, SECTOR_BITS = 8, 8


def plan_kernel(*refs):
    mark_refs = refs[:X]
    plan_ref, picked_ref, label_ref, sem = refs[X:]
    me = lax.axis_index("sector")
    my_x = me // Y
    rows, cols = Y * X * 16, 128
    marks = jnp.concatenate([r[...].reshape(Y * 16, cols) for r in mark_refs])
    marks = marks.astype(jnp.float32).astype(jnp.int32)
    s = lax.broadcasted_iota(jnp.int32, (rows, cols), 0) & 15
    k = lax.broadcasted_iota(jnp.int32, (rows, cols), 1)
    mine = ((marks >> 3) == me) & (s < 8) & (k < 8)
    ones = jnp.where(mine, 1.0, 0.0)
    flags = ones.astype(jnp.bfloat16)
    i = lax.broadcasted_iota(jnp.int32, (cols, cols), 0)
    j = lax.broadcasted_iota(jnp.int32, (cols, cols), 1)
    earlier = jnp.where(i < j, 1.0, 0.0).astype(jnp.bfloat16)
    position = jnp.dot(flags, earlier, preferred_element_type=jnp.float32)
    per_row = jnp.broadcast_to(jnp.sum(ones, axis=1, keepdims=True), (rows, cols))
    per_row = per_row.astype(jnp.bfloat16)
    above = jnp.where((i > j) & ((i >> 4) == (j >> 4)), 1.0, 0.0).astype(jnp.bfloat16)
    before = [
        jnp.dot(above, per_row[n : n + cols], preferred_element_type=jnp.float32)
        for n in range(0, rows, cols)
    ]
    position = position + jnp.concatenate(before)
    label = ((s << 6) | ((marks & 7) << 3) | k).astype(jnp.float32) + 1.0
    lane = lax.broadcasted_iota(jnp.int32, (X * Y, cols), 1)
    picked = jnp.zeros((X * Y, cols), jnp.float32)
    for n in range(CAP):
        chosen = jnp.where(mine & (position == float(n)), label, 0.0)
        chosen = jnp.sum(jnp.sum(chosen.reshape(X * Y, 16, cols), axis=1), axis=1, keepdims=True)
        picked = picked + jnp.where(lane == n, chosen, 0.0)
    picked_ref[...] = picked.astype(jnp.int32) - 1
    copy = pltpu.make_async_copy(picked_ref, label_ref, sem)
    copy.start()
    copy.wait()

    def note(device, count):
        base = (((my_x - (device >> 3)) & (X - 1)) << 5) | ((device & 7) << 2)
        for n in range(CAP):
            label = label_ref[device, n]
            sector = (device << 3) | (label >> 6)
            plan_ref[count] = (((base | n) << SECTOR_BITS | sector) << GROUP_BITS) | (label & 63)
            count = count + jnp.where(label >= 0, 1, 0)
        return count

    count = lax.fori_loop(0, X * Y, note, 0)
    for extra in range(UNROLL - 1):
        plan_ref[count + extra] = 64
    plan_ref[PLAN - 1] = (count + UNROLL - 1) // UNROLL


PLAN = X * Y * CAP + 16
PICKED = X * Y * CAP


def make_plan(marks):
    return pl.pallas_call(
        plan_kernel,
        out_shape=jax.ShapeDtypeStruct((PLAN,), jnp.int32),
        in_specs=[VMEM] * X,
        out_specs=SMEM,
        scratch_shapes=[
            pltpu.VMEM((X * Y, 128), jnp.int32),
            pltpu.SMEM((X * Y, 128), jnp.int32),
            pltpu.SemaphoreType.DMA,
        ],
        compiler_params=pltpu.CompilerParams(vmem_limit_bytes=16 * 2**20),
        name="plan_slots",
    )(*marks)


def half_products(plan_ref, arrived_hbm, left_hbm, wave_of, arrived_ref, left_ref, grouped_ref, sems, pieces_here=None):
    copies = [
        pltpu.make_async_copy(arrived_hbm, arrived_ref, sems.at[0]),
        pltpu.make_async_copy(left_hbm, left_ref, sems.at[1]),
    ]
    for copy in copies:
        copy.start()
    terms = left_ref.shape[0]
    width = arrived_ref.shape[1]

    def clear(g, carry):
        for n in range(8):
            grouped_ref[g * 8 + n] = jnp.zeros((width, width), jnp.float32)
        return carry

    lax.fori_loop(0, terms // 8, clear, 0)
    for copy in copies:
        copy.wait()
    if pieces_here is not None:
        pieces_here()

    def some(step, carry):
        waves = []
        groups = []
        for i in range(UNROLL):
            entry = plan_ref[step * UNROLL + i]
            groups.append(entry & (2**GROUP_BITS - 1))
            sector = (entry >> GROUP_BITS) & (2**SECTOR_BITS - 1)
            slot = entry >> (GROUP_BITS + SECTOR_BITS)
            wave = lax.dot_general(
                wave_of(step * UNROLL + i, sector).reshape(width, width),
                arrived_ref[slot],
                (((1,), (1,)), ((), ())),
                preferred_element_type=jnp.float32,
            )
            waves.append(wave.astype(jnp.bfloat16))
        for group, wave in zip(groups, waves):
            grouped_ref[group] = grouped_ref[group] + wave.astype(jnp.float32)
        return carry

    lax.fori_loop(0, plan_ref[PLAN - 1], some, 0)


def left_sum(left_ref, grouped_ref, t):
    lefts = jnp.concatenate([left_ref[t * 8 + k] for k in range(8)], axis=1)
    groups = jnp.concatenate(
        [grouped_ref[t * 8 + k].astype(jnp.bfloat16) for k in range(8)], axis=0
    )
    return jnp.dot(lefts, groups, preferred_element_type=jnp.float32)


def own_kernel(places, plan_ref, other_plan_ref, arrived_hbm, left_hbm, *refs):
    piece_refs = refs[: len(places)]
    sums_ref, picked_ref, wave_ref, arrived_ref, left_ref, grouped_ref, sems, piece_sems = refs[
        len(places) :
    ]
    op = lax.axis_index("op")
    sign = 1 - 2 * lax.rem(op, CORES)
    copies = []
    for i, (base, step) in enumerate(places):
        piece = lax.rem(op // CORES - step * sign + Z, Z)
        copies.append(
            pltpu.make_async_copy(
                piece_refs[i],
                wave_ref.at[pl.ds(base, piece_refs[i].shape[0]), piece],
                piece_sems.at[i],
            )
        )
    for copy in copies:
        copy.start()

    def pieces_here():
        for copy in copies:
            copy.wait()

    half_products(
        plan_ref,
        arrived_hbm,
        left_hbm,
        lambda n, sector: wave_ref[sector],
        arrived_ref,
        left_ref,
        grouped_ref,
        sems,
        pieces_here,
    )

    def pick(step, carry):
        for i in range(UNROLL):
            n = step * UNROLL + i
            picked_ref[n] = wave_ref[(other_plan_ref[n] >> GROUP_BITS) & (2**SECTOR_BITS - 1)]
        return carry

    lax.fori_loop(0, other_plan_ref[PLAN - 1], pick, 0)

    def left(pair, carry):
        for j in range(2):
            sums_ref[pair * 2 + j] = left_sum(left_ref, grouped_ref, pair * 2 + j)
        return carry

    lax.fori_loop(0, 4, left, 0)


def other_kernel(
    plan_ref,
    arrived_hbm,
    left_hbm,
    picked_hbm,
    sums_hbm,
    out_ref,
    arrived_ref,
    left_ref,
    grouped_ref,
    sems,
    picked_ref,
    sums_ref,
    more_sems,
):
    copies = [
        pltpu.make_async_copy(picked_hbm, picked_ref, more_sems.at[0]),
        pltpu.make_async_copy(sums_hbm, sums_ref, more_sems.at[1]),
    ]
    for copy in copies:
        copy.start()

    def more_here():
        for copy in copies:
            copy.wait()

    half_products(
        plan_ref,
        arrived_hbm,
        left_hbm,
        lambda n, sector: picked_ref[n],
        arrived_ref,
        left_ref,
        grouped_ref,
        sems,
        more_here,
    )
    width = sums_ref.shape[2]

    def left(pair, carry):
        both = []
        for j in range(2):
            t = pair * 2 + j
            total = sums_ref[t] + left_sum(left_ref, grouped_ref, t)
            both.append(total.reshape(16, 8, width))
        rows = jnp.stack(both, axis=1).reshape(16, 16, width)
        out_ref[:, pl.ds(pl.multiple_of(pair * 16, 16), 16), :] = rows.astype(out_ref.dtype)
        return carry

    lax.fori_loop(0, 4, left, 0)


SMEM = pl.BlockSpec(memory_space=pltpu.SMEM)
VMEM = pl.BlockSpec(memory_space=pltpu.VMEM)
HBM = pl.BlockSpec(memory_space=pl.ANY)


def work_space(arrived, left):
    slots, width, _ = arrived.shape
    terms = left.shape[0]
    return [
        pltpu.VMEM((slots, width, width), jnp.bfloat16),
        pltpu.VMEM((terms, width, width), jnp.bfloat16),
        pltpu.VMEM((terms + 1, width, width), jnp.float32),
        pltpu.SemaphoreType.DMA((2,)),
    ]


COST = pl.CostEstimate(flops=2 * 128 * 128**3, bytes_accessed=16 * 2**20, transcendentals=0)


def own_products(plan, other_plan, arrived, left, pieces):
    width = arrived.shape[1]
    count = len(pieces)
    return pl.pallas_call(
        functools.partial(own_kernel, [p[1:] for p in pieces]),
        out_shape=(
            jax.ShapeDtypeStruct((8, width, width), jnp.float32),
            jax.ShapeDtypeStruct((PICKED, Z, 16, width), jnp.bfloat16),
        ),
        in_specs=[SMEM, SMEM] + [HBM] * (2 + count),
        out_specs=(VMEM, VMEM),
        scratch_shapes=[pltpu.VMEM((X * Y * 8, Z, 16, width), jnp.bfloat16)]
        + work_space(arrived, left)
        + [pltpu.SemaphoreType.DMA((count,))],
        compiler_params=pltpu.CompilerParams(vmem_limit_bytes=60 * 2**20),
        cost_estimate=COST,
        name="own_products",
    )(plan, other_plan, arrived, left, *[p[0] for p in pieces])


def other_products(plan, arrived, left, picked, sums):
    width = arrived.shape[1]
    return pl.pallas_call(
        other_kernel,
        out_shape=jax.ShapeDtypeStruct((16, 64, width), jnp.bfloat16),
        in_specs=[SMEM, HBM, HBM, HBM, HBM],
        out_specs=VMEM,
        scratch_shapes=work_space(arrived, left)
        + [
            pltpu.VMEM(picked.shape, picked.dtype),
            pltpu.VMEM(sums.shape, sums.dtype),
            pltpu.SemaphoreType.DMA((2,)),
        ],
        compiler_params=pltpu.CompilerParams(vmem_limit_bytes=32 * 2**20),
        cost_estimate=COST,
        name="other_products",
    )(plan, arrived, left, picked, sums)


def spread_column(wavefunction, targets):
    op = lax.axis_index("op")
    _, sectors, rows, cols = wavefunction.shape
    piece = lax.dynamic_slice(
        wavefunction, (op % CORES, 0, (op // CORES) * 16, 0), (1, sectors, 16, cols)
    )
    marks = jnp.pad(targets.astype(jnp.bfloat16), ((0, 16 - sectors), (0, cols - targets.shape[1])))
    load = jnp.concatenate([piece, marks[None, None]], axis=1)
    columns = [[x * Y + y for y in range(Y)] for x in range(X)]
    return lax.all_to_all(
        jnp.broadcast_to(load, (Y,) + load.shape[1:]),
        "sector",
        split_axis=0,
        concat_axis=0,
        axis_index_groups=columns,
        tiled=True,
    )


def per_device(wavefunction, right_blocks, left_blocks, targets):
    sectors, terms, width, _ = right_blocks.shape
    pairs = sectors * terms
    groups = lax.axis_size("sector")
    swap = functools.partial(lax.ppermute, axis_name="op", perm=core_swap())
    ring = functools.partial(lax.ppermute, axis_name="op", perm=z_ring())
    tie = lax.optimization_barrier
    packed = pack(targets, right_blocks, groups)
    column = spread_column(wavefunction, targets)
    columns = [column] + [lax.ppermute(column, "sector", x_shift(d)) for d in range(1, X)]
    packed, *columns = tie((packed, *columns))
    arrived = lax.all_to_all(packed, "sector", split_axis=0, concat_axis=0, tiled=True)
    own_left = left_blocks.reshape(pairs, width, width)

    size = Y * sectors
    own_plan = make_plan([c[:, sectors] for c in columns])
    blocks = [c[:, :sectors].reshape(size, 16, width) for c in columns]
    chains = [[jnp.concatenate(blocks[:2])], [jnp.concatenate(blocks[2:])]]
    for step in range(1, Z):
        for chain in chains:
            chain.append(ring(chain[-1]))
        if step == 1:
            chains[0][1], own_plan, own_left = tie((chains[0][1], own_plan, own_left))
            other_plan = swap(own_plan)
            other_left = swap(own_left)
        if step == 4:
            chains[0][4], other_plan, other_left = tie((chains[0][4], other_plan, other_left))
    pieces = []
    for base, chain in ((0, chains[0]), (2 * size, chains[1])):
        pieces += [(block, base, step) for step, block in enumerate(chain)]

    arrived, *_ = tie((arrived, chains[0][-1], chains[1][-1]))
    other_arrived = swap(arrived)
    sums, picked = own_products(own_plan, other_plan, arrived, own_left, pieces)
    partial_value = other_products(other_plan, other_arrived, other_left, picked, sums)
    got = lax.all_to_all(partial_value, "op", split_axis=0, concat_axis=0, tiled=True)
    return jnp.sum(got.reshape(Z, CORES, 8, 8, width).astype(jnp.float32), axis=0)


def solution(mesh):
    return jax.shard_map(
        per_device,
        mesh=mesh,
        in_specs=(
            P(None, "sector", None, None),
            P("sector", "op", None, None),
            P("sector", "op", None, None),
            P("sector", "op"),
        ),
        out_specs=P(None, "sector", "op", None),
        check_vma=False,
    )
```

```python
import functools

import jax
import jax.numpy as jnp
from jax import lax
from jax.experimental import pallas as pl
from jax.experimental.pallas import tpu as pltpu
from jax.sharding import PartitionSpec as P

X, Y, Z, CORES = 4, 8, 8, 2
CAP = 4


def z_shift(distance):
    return [
        (z * CORES + c, ((z + distance) % Z) * CORES + c) for z in range(Z) for c in range(CORES)
    ]


def core_swap():
    return [(z * CORES + c, z * CORES + 1 - c) for z in range(Z) for c in range(CORES)]


def x_shift(distance):
    return [(x * Y + y, ((x + distance) % X) * Y + y) for x in range(X) for y in range(Y)]


def pack_kernel(targets_ref, right_ref, packed_ref, counts_ref):
    groups = counts_ref.shape[0]
    sectors, terms = targets_ref.shape

    def clear(g, carry):
        counts_ref[g] = 0
        return carry

    lax.fori_loop(0, groups, clear, 0)

    def place(s, carry):
        for k in range(terms):
            owner = targets_ref[s, k] >> 3
            position = counts_ref[owner]
            counts_ref[owner] = position + 1
            packed_ref[owner * CAP + position] = right_ref[s, k]
        return carry

    lax.fori_loop(0, sectors, place, 0)


def pack(targets, right_blocks, groups):
    _, _, rows, cols = right_blocks.shape
    return pl.pallas_call(
        pack_kernel,
        out_shape=jax.ShapeDtypeStruct((groups * CAP, rows, cols), right_blocks.dtype),
        in_specs=[
            pl.BlockSpec(memory_space=pltpu.SMEM),
            pl.BlockSpec(memory_space=pltpu.VMEM),
        ],
        out_specs=pl.BlockSpec(memory_space=pltpu.VMEM),
        scratch_shapes=[pltpu.SMEM((groups,), jnp.int32)],
        compiler_params=pltpu.CompilerParams(vmem_limit_bytes=16 * 2**20),
        cost_estimate=pl.CostEstimate(flops=0, bytes_accessed=8 * 2**20, transcendentals=0),
        name="pack_blocks",
    )(targets, right_blocks)


UNROLL = 16
GROUP_BITS, SECTOR_BITS = 8, 8


def plan_kernel(*refs):
    mark_refs = refs[:X]
    plan_ref, picked_ref, label_ref, sem = refs[X:]
    me = lax.axis_index("sector")
    my_x = me // Y
    rows, cols = Y * X * 16, 128
    marks = jnp.concatenate([r[...].reshape(Y * 16, cols) for r in mark_refs])
    marks = marks.astype(jnp.float32).astype(jnp.int32)
    s = lax.broadcasted_iota(jnp.int32, (rows, cols), 0) & 15
    k = lax.broadcasted_iota(jnp.int32, (rows, cols), 1)
    mine = ((marks >> 3) == me) & (s < 8) & (k < 8)
    ones = jnp.where(mine, 1.0, 0.0)
    flags = ones.astype(jnp.bfloat16)
    i = lax.broadcasted_iota(jnp.int32, (cols, cols), 0)
    j = lax.broadcasted_iota(jnp.int32, (cols, cols), 1)
    earlier = jnp.where(i < j, 1.0, 0.0).astype(jnp.bfloat16)
    position = jnp.dot(flags, earlier, preferred_element_type=jnp.float32)
    per_row = jnp.broadcast_to(jnp.sum(ones, axis=1, keepdims=True), (rows, cols))
    per_row = per_row.astype(jnp.bfloat16)
    above = jnp.where((i > j) & ((i >> 4) == (j >> 4)), 1.0, 0.0).astype(jnp.bfloat16)
    before = [
        jnp.dot(above, per_row[n : n + cols], preferred_element_type=jnp.float32)
        for n in range(0, rows, cols)
    ]
    position = position + jnp.concatenate(before)
    label = ((s << 6) | ((marks & 7) << 3) | k).astype(jnp.float32) + 1.0
    lane = lax.broadcasted_iota(jnp.int32, (X * Y, cols), 1)
    picked = jnp.zeros((X * Y, cols), jnp.float32)
    for n in range(CAP):
        chosen = jnp.where(mine & (position == float(n)), label, 0.0)
        chosen = jnp.sum(jnp.sum(chosen.reshape(X * Y, 16, cols), axis=1), axis=1, keepdims=True)
        picked = picked + jnp.where(lane == n, chosen, 0.0)
    picked_ref[...] = picked.astype(jnp.int32) - 1
    copy = pltpu.make_async_copy(picked_ref, label_ref, sem)
    copy.start()
    copy.wait()

    def note(device, count):
        base = (((my_x - (device >> 3)) & (X - 1)) << 5) | ((device & 7) << 2)
        for n in range(CAP):
            label = label_ref[device, n]
            sector = (device << 3) | (label >> 6)
            plan_ref[count] = (((base | n) << SECTOR_BITS | sector) << GROUP_BITS) | (label & 63)
            count = count + jnp.where(label >= 0, 1, 0)
        return count

    count = lax.fori_loop(0, X * Y, note, 0)
    for extra in range(UNROLL - 1):
        plan_ref[count + extra] = 64
    plan_ref[PLAN - 1] = (count + UNROLL - 1) // UNROLL


PLAN = X * Y * CAP + 16
PICKED = X * Y * CAP


def make_plan(marks):
    return pl.pallas_call(
        plan_kernel,
        out_shape=jax.ShapeDtypeStruct((PLAN,), jnp.int32),
        in_specs=[VMEM] * X,
        out_specs=SMEM,
        scratch_shapes=[
            pltpu.VMEM((X * Y, 128), jnp.int32),
            pltpu.SMEM((X * Y, 128), jnp.int32),
            pltpu.SemaphoreType.DMA,
        ],
        compiler_params=pltpu.CompilerParams(vmem_limit_bytes=16 * 2**20),
        name="plan_slots",
    )(*marks)


def half_products(
    plan_ref, arrived_hbm, left_hbm, wave_of, arrived_ref, left_ref, grouped_ref, sems, wait_first, wait_step, start_more=None
):
    arrived = pltpu.make_async_copy(arrived_hbm, arrived_ref, sems.at[0])
    left = pltpu.make_async_copy(left_hbm, left_ref, sems.at[1])
    arrived.start()
    if start_more is not None:
        start_more()
    left.start()
    terms = left_ref.shape[0]
    width = arrived_ref.shape[1]

    def clear(g, carry):
        for n in range(8):
            grouped_ref[g * 8 + n] = jnp.zeros((width, width), jnp.float32)
        return carry

    lax.fori_loop(0, terms // 8, clear, 0)
    wait_first()
    arrived.wait()

    def some(step, carry):
        wait_step(step)
        waves = []
        groups = []
        for i in range(UNROLL):
            entry = plan_ref[step * UNROLL + i]
            groups.append(entry & (2**GROUP_BITS - 1))
            sector = (entry >> GROUP_BITS) & (2**SECTOR_BITS - 1)
            slot = entry >> (GROUP_BITS + SECTOR_BITS)
            wave = lax.dot_general(
                wave_of(step * UNROLL + i, sector).reshape(width, width),
                arrived_ref[slot],
                (((1,), (1,)), ((), ())),
                preferred_element_type=jnp.float32,
            )
            waves.append(wave.astype(jnp.bfloat16))
        for group, wave in zip(groups, waves):
            grouped_ref[group] = grouped_ref[group] + wave.astype(jnp.float32)
        return carry

    lax.fori_loop(0, plan_ref[PLAN - 1], some, 0)
    left.wait()


def left_sum(left_ref, grouped_ref, t):
    lefts = jnp.concatenate([left_ref[t * 8 + k] for k in range(8)], axis=1)
    groups = jnp.concatenate(
        [grouped_ref[t * 8 + k].astype(jnp.bfloat16) for k in range(8)], axis=0
    )
    return jnp.dot(lefts, groups, preferred_element_type=jnp.float32)


def own_kernel(places, plan_ref, other_plan_ref, arrived_hbm, left_hbm, *refs):
    piece_refs = refs[: len(places)]
    (
        sums_ref,
        picked_hbm,
        picked_ref,
        wave_ref,
        arrived_ref,
        left_ref,
        grouped_ref,
        sems,
        piece_sems,
        picked_sems,
    ) = refs[len(places) :]
    op = lax.axis_index("op")
    copies = []
    for i, (base, step) in enumerate(places):
        piece = lax.rem(op // CORES - step + Z, Z)
        copies.append(
            pltpu.make_async_copy(
                piece_refs[i],
                wave_ref.at[pl.ds(base, piece_refs[i].shape[0]), piece],
                piece_sems.at[i],
            )
        )
    for copy in copies:
        copy.start()

    def picked_copy(step):
        rows = pl.ds(step * UNROLL, UNROLL)
        return pltpu.make_async_copy(picked_ref.at[rows], picked_hbm.at[rows], picked_sems.at[step])

    def pick(step, carry):
        for i in range(UNROLL):
            n = step * UNROLL + i
            picked_ref[n] = wave_ref[(other_plan_ref[n] >> GROUP_BITS) & (2**SECTOR_BITS - 1)]
        picked_copy(step).start()
        return carry

    def finish_pick(step, carry):
        picked_copy(step).wait()
        return carry

    other_steps = other_plan_ref[PLAN - 1]

    def pieces_here():
        for copy in copies:
            copy.wait()
        lax.fori_loop(0, other_steps, pick, 0)

    half_products(
        plan_ref,
        arrived_hbm,
        left_hbm,
        lambda n, sector: wave_ref[sector],
        arrived_ref,
        left_ref,
        grouped_ref,
        sems,
        pieces_here,
        lambda step: None,
    )

    def left(pair, carry):
        for j in range(2):
            sums_ref[pair * 2 + j] = left_sum(left_ref, grouped_ref, pair * 2 + j)
        return carry

    lax.fori_loop(0, 4, left, 0)
    lax.fori_loop(0, other_steps, finish_pick, 0)


def other_kernel(
    plan_ref,
    arrived_hbm,
    left_hbm,
    picked_hbm,
    sums_hbm,
    out_ref,
    arrived_ref,
    left_ref,
    grouped_ref,
    sems,
    picked_ref,
    sums_ref,
    more_sems,
):
    sums_copy = pltpu.make_async_copy(sums_hbm, sums_ref, more_sems.at[PICKED // UNROLL])
    steps = plan_ref[PLAN - 1]

    def picked_copy(step):
        rows = pl.ds(step * UNROLL, UNROLL)
        return pltpu.make_async_copy(picked_hbm.at[rows], picked_ref.at[rows], more_sems.at[step])

    def start_step(step, carry):
        picked_copy(step).start()
        return carry

    def start_more():
        lax.fori_loop(0, steps, start_step, 0)
        sums_copy.start()

    def wait_step(step):
        picked_copy(step).wait()

    half_products(
        plan_ref,
        arrived_hbm,
        left_hbm,
        lambda n, sector: picked_ref[n],
        arrived_ref,
        left_ref,
        grouped_ref,
        sems,
        lambda: None,
        wait_step,
        start_more,
    )
    sums_copy.wait()
    width = sums_ref.shape[2]

    def left(pair, carry):
        both = []
        for j in range(2):
            t = pair * 2 + j
            total = sums_ref[t] + left_sum(left_ref, grouped_ref, t)
            both.append(total.reshape(16, 8, width))
        rows = jnp.stack(both, axis=1).reshape(16, 16, width)
        out_ref[:, pl.ds(pl.multiple_of(pair * 16, 16), 16), :] = rows.astype(out_ref.dtype)
        return carry

    lax.fori_loop(0, 4, left, 0)


SMEM = pl.BlockSpec(memory_space=pltpu.SMEM)
VMEM = pl.BlockSpec(memory_space=pltpu.VMEM)
HBM = pl.BlockSpec(memory_space=pl.ANY)


def work_space(arrived, left):
    slots, width, _ = arrived.shape
    terms = left.shape[0]
    return [
        pltpu.VMEM((slots, width, width), jnp.bfloat16),
        pltpu.VMEM((terms, width, width), jnp.bfloat16),
        pltpu.VMEM((terms + 1, width, width), jnp.float32),
        pltpu.SemaphoreType.DMA((2,)),
    ]


COST = pl.CostEstimate(flops=2 * 128 * 128**3, bytes_accessed=16 * 2**20, transcendentals=0)


def own_products(plan, other_plan, arrived, left, pieces):
    width = arrived.shape[1]
    count = len(pieces)
    return pl.pallas_call(
        functools.partial(own_kernel, [p[1:] for p in pieces]),
        out_shape=(
            jax.ShapeDtypeStruct((8, width, width), jnp.float32),
            jax.ShapeDtypeStruct((PICKED, Z, 16, width), jnp.bfloat16),
        ),
        in_specs=[SMEM, SMEM] + [HBM] * (2 + count),
        out_specs=(VMEM, HBM),
        scratch_shapes=[
            pltpu.VMEM((PICKED, Z, 16, width), jnp.bfloat16),
            pltpu.VMEM((X * Y * 8, Z, 16, width), jnp.bfloat16),
        ]
        + work_space(arrived, left)
        + [
            pltpu.SemaphoreType.DMA((count,)),
            pltpu.SemaphoreType.DMA((PICKED // UNROLL,)),
        ],
        compiler_params=pltpu.CompilerParams(vmem_limit_bytes=60 * 2**20),
        cost_estimate=COST,
        name="own_products",
    )(plan, other_plan, arrived, left, *[p[0] for p in pieces])


def other_products(plan, arrived, left, picked, sums):
    width = arrived.shape[1]
    return pl.pallas_call(
        other_kernel,
        out_shape=jax.ShapeDtypeStruct((16, 64, width), jnp.bfloat16),
        in_specs=[SMEM, HBM, HBM, HBM, HBM],
        out_specs=VMEM,
        scratch_shapes=work_space(arrived, left)
        + [
            pltpu.VMEM(picked.shape, picked.dtype),
            pltpu.VMEM(sums.shape, sums.dtype),
            pltpu.SemaphoreType.DMA((PICKED // UNROLL + 1,)),
        ],
        compiler_params=pltpu.CompilerParams(vmem_limit_bytes=60 * 2**20),
        cost_estimate=COST,
        name="other_products",
    )(plan, arrived, left, picked, sums)


def spread_column(wavefunction, targets):
    op = lax.axis_index("op")
    _, sectors, rows, cols = wavefunction.shape
    piece = lax.dynamic_slice(
        wavefunction, (op % CORES, 0, (op // CORES) * 16, 0), (1, sectors, 16, cols)
    )
    marks = jnp.pad(targets.astype(jnp.bfloat16), ((0, 16 - sectors), (0, cols - targets.shape[1])))
    load = jnp.concatenate([piece, marks[None, None]], axis=1)
    columns = [[x * Y + y for y in range(Y)] for x in range(X)]
    return lax.all_to_all(
        jnp.broadcast_to(load, (Y,) + load.shape[1:]),
        "sector",
        split_axis=0,
        concat_axis=0,
        axis_index_groups=columns,
        tiled=True,
    )


def per_device(wavefunction, right_blocks, left_blocks, targets):
    sectors, terms, width, _ = right_blocks.shape
    pairs = sectors * terms
    groups = lax.axis_size("sector")
    swap = functools.partial(lax.ppermute, axis_name="op", perm=core_swap())
    ring_up = functools.partial(lax.ppermute, axis_name="op", perm=z_shift(1))
    ring_down = functools.partial(lax.ppermute, axis_name="op", perm=z_shift(-1))
    tie = lax.optimization_barrier
    packed = pack(targets, right_blocks, groups)
    column = spread_column(wavefunction, targets)
    columns = [column] + [lax.ppermute(column, "sector", x_shift(d)) for d in range(1, X)]
    packed, *_ = tie((packed, *columns))
    arrived = lax.all_to_all(packed, "sector", split_axis=0, concat_axis=0, tiled=True)
    own_left = left_blocks.reshape(pairs, width, width)

    size = Y * sectors
    own_plan = make_plan([c[:, sectors] for c in columns])
    blocks = [c[:, :sectors].reshape(size, 16, width) for c in columns]
    starts = [jnp.concatenate(blocks[:2]), jnp.concatenate(blocks[2:])]
    ups = [[s] for s in starts]
    downs = [[s] for s in starts]
    for step in range(1, Z // 2):
        for chain in ups:
            chain.append(ring_up(chain[-1]))
        for chain in downs:
            chain.append(ring_down(chain[-1]))
        if step == 2:
            ups[1][2], own_left = tie((ups[1][2], own_left))
            other_left = swap(own_left)
        if step == 3:
            ups[0][3], other_plan = tie((ups[0][3], swap(own_plan)))
    pieces = []
    last = []
    for n, start in enumerate(starts):
        base = 2 * size * n
        pieces.append((start, base, 0))
        for step in range(1, Z // 2):
            pieces.append((ups[n][step], base, step))
            pieces.append((downs[n][step], base, -step))
        last.append((ring_up(ups[n][-1][:size]), base, Z // 2))
        last.append((ring_down(downs[n][-1][size:]), base + size, Z // 2))
    pieces += last

    arrived, *_ = tie((arrived, *[p[0] for p in last]))
    other_arrived = swap(arrived)
    sums, picked = own_products(own_plan, other_plan, arrived, own_left, pieces)
    partial_value = other_products(other_plan, other_arrived, other_left, picked, sums)
    got = lax.all_to_all(partial_value, "op", split_axis=0, concat_axis=0, tiled=True)
    return jnp.sum(got.reshape(Z, CORES, 8, 8, width).astype(jnp.float32), axis=0)


def solution(mesh):
    return jax.shard_map(
        per_device,
        mesh=mesh,
        in_specs=(
            P(None, "sector", None, None),
            P("sector", "op", None, None),
            P("sector", "op", None, None),
            P("sector", "op"),
        ),
        out_specs=P(None, "sector", "op", None),
        check_vma=False,
    )
```

```python
import functools

import jax
import jax.numpy as jnp
from jax import lax
from jax.experimental import pallas as pl
from jax.experimental.pallas import tpu as pltpu
from jax.sharding import PartitionSpec as P

X, Y, Z, CORES = 4, 8, 8, 2
CAP = 4


def z_shift(distance):
    return [
        (z * CORES + c, ((z + distance) % Z) * CORES + c) for z in range(Z) for c in range(CORES)
    ]


def core_swap():
    return [(z * CORES + c, z * CORES + 1 - c) for z in range(Z) for c in range(CORES)]


def x_shift(distance):
    return [(x * Y + y, ((x + distance) % X) * Y + y) for x in range(X) for y in range(Y)]


def pack_kernel(targets_ref, right_ref, packed_ref, counts_ref):
    groups = counts_ref.shape[0]
    sectors, terms = targets_ref.shape

    def clear(g, carry):
        counts_ref[g] = 0
        return carry

    lax.fori_loop(0, groups, clear, 0)

    def place(s, carry):
        for k in range(terms):
            owner = targets_ref[s, k] >> 3
            position = counts_ref[owner]
            counts_ref[owner] = position + 1
            packed_ref[owner * CAP + position] = right_ref[s, k]
        return carry

    lax.fori_loop(0, sectors, place, 0)


def pack(targets, right_blocks, groups):
    _, _, rows, cols = right_blocks.shape
    return pl.pallas_call(
        pack_kernel,
        out_shape=jax.ShapeDtypeStruct((groups * CAP, rows, cols), right_blocks.dtype),
        in_specs=[
            pl.BlockSpec(memory_space=pltpu.SMEM),
            pl.BlockSpec(memory_space=pltpu.VMEM),
        ],
        out_specs=pl.BlockSpec(memory_space=pltpu.VMEM),
        scratch_shapes=[pltpu.SMEM((groups,), jnp.int32)],
        compiler_params=pltpu.CompilerParams(vmem_limit_bytes=16 * 2**20),
        cost_estimate=pl.CostEstimate(flops=0, bytes_accessed=8 * 2**20, transcendentals=0),
        name="pack_blocks",
    )(targets, right_blocks)


UNROLL = 16
GROUP_BITS, SECTOR_BITS = 8, 8


def plan_kernel(*refs):
    mark_refs = refs[:X]
    plan_ref, picked_ref, label_ref, sem = refs[X:]
    me = lax.axis_index("sector")
    my_x = me // Y
    rows, cols = Y * X * 16, 128
    marks = jnp.concatenate([r[...].reshape(Y * 16, cols) for r in mark_refs])
    marks = marks.astype(jnp.float32).astype(jnp.int32)
    s = lax.broadcasted_iota(jnp.int32, (rows, cols), 0) & 15
    k = lax.broadcasted_iota(jnp.int32, (rows, cols), 1)
    mine = ((marks >> 3) == me) & (s < 8) & (k < 8)
    ones = jnp.where(mine, 1.0, 0.0)
    flags = ones.astype(jnp.bfloat16)
    i = lax.broadcasted_iota(jnp.int32, (cols, cols), 0)
    j = lax.broadcasted_iota(jnp.int32, (cols, cols), 1)
    earlier = jnp.where(i < j, 1.0, 0.0).astype(jnp.bfloat16)
    position = jnp.dot(flags, earlier, preferred_element_type=jnp.float32)
    per_row = jnp.broadcast_to(jnp.sum(ones, axis=1, keepdims=True), (rows, cols))
    per_row = per_row.astype(jnp.bfloat16)
    above = jnp.where((i > j) & ((i >> 4) == (j >> 4)), 1.0, 0.0).astype(jnp.bfloat16)
    before = [
        jnp.dot(above, per_row[n : n + cols], preferred_element_type=jnp.float32)
        for n in range(0, rows, cols)
    ]
    position = position + jnp.concatenate(before)
    label = ((s << 6) | ((marks & 7) << 3) | k).astype(jnp.float32) + 1.0
    lane = lax.broadcasted_iota(jnp.int32, (X * Y, cols), 1)
    picked = jnp.zeros((X * Y, cols), jnp.float32)
    for n in range(CAP):
        chosen = jnp.where(mine & (position == float(n)), label, 0.0)
        chosen = jnp.sum(jnp.sum(chosen.reshape(X * Y, 16, cols), axis=1), axis=1, keepdims=True)
        picked = picked + jnp.where(lane == n, chosen, 0.0)
    picked_ref[...] = picked.astype(jnp.int32) - 1
    copy = pltpu.make_async_copy(picked_ref, label_ref, sem)
    copy.start()
    copy.wait()

    def note(device, count):
        base = (((my_x - (device >> 3)) & (X - 1)) << 5) | ((device & 7) << 2)
        for n in range(CAP):
            label = label_ref[device, n]
            sector = (device << 3) | (label >> 6)
            plan_ref[count] = (((base | n) << SECTOR_BITS | sector) << GROUP_BITS) | (label & 63)
            count = count + jnp.where(label >= 0, 1, 0)
        return count

    count = lax.fori_loop(0, X * Y, note, 0)
    for extra in range(UNROLL - 1):
        plan_ref[count + extra] = 64
    plan_ref[PLAN - 1] = (count + UNROLL - 1) // UNROLL


PLAN = X * Y * CAP + 16
PICKED = X * Y * CAP


def make_plan(marks):
    return pl.pallas_call(
        plan_kernel,
        out_shape=jax.ShapeDtypeStruct((PLAN,), jnp.int32),
        in_specs=[VMEM] * X,
        out_specs=SMEM,
        scratch_shapes=[
            pltpu.VMEM((X * Y, 128), jnp.int32),
            pltpu.SMEM((X * Y, 128), jnp.int32),
            pltpu.SemaphoreType.DMA,
        ],
        compiler_params=pltpu.CompilerParams(vmem_limit_bytes=16 * 2**20),
        name="plan_slots",
    )(*marks)


def half_products(
    plan_ref, arrived_hbm, left_hbm, wave_of, arrived_ref, left_ref, grouped_ref, sems, wait_first, wait_step, start_more=None
):
    arrived = pltpu.make_async_copy(arrived_hbm, arrived_ref, sems.at[0])
    left = pltpu.make_async_copy(left_hbm, left_ref, sems.at[1])
    arrived.start()
    if start_more is not None:
        start_more()
    left.start()
    terms = left_ref.shape[0]
    width = arrived_ref.shape[1]

    def clear(g, carry):
        for n in range(8):
            grouped_ref[g * 8 + n] = jnp.zeros((width, width), jnp.float32)
        return carry

    lax.fori_loop(0, terms // 8, clear, 0)
    wait_first()
    arrived.wait()

    def some(step, carry):
        wait_step(step)
        waves = []
        groups = []
        for i in range(UNROLL):
            entry = plan_ref[step * UNROLL + i]
            groups.append(entry & (2**GROUP_BITS - 1))
            sector = (entry >> GROUP_BITS) & (2**SECTOR_BITS - 1)
            slot = entry >> (GROUP_BITS + SECTOR_BITS)
            wave = lax.dot_general(
                wave_of(step * UNROLL + i, sector).reshape(width, width),
                arrived_ref[slot],
                (((1,), (1,)), ((), ())),
                preferred_element_type=jnp.float32,
            )
            waves.append(wave.astype(jnp.bfloat16))
        for group, wave in zip(groups, waves):
            grouped_ref[group] = grouped_ref[group] + wave.astype(jnp.float32)
        return carry

    lax.fori_loop(0, plan_ref[PLAN - 1], some, 0)
    left.wait()


def left_sum(left_ref, grouped_ref, t):
    lefts = jnp.concatenate([left_ref[t * 8 + k] for k in range(8)], axis=1)
    groups = jnp.concatenate(
        [grouped_ref[t * 8 + k].astype(jnp.bfloat16) for k in range(8)], axis=0
    )
    return jnp.dot(lefts, groups, preferred_element_type=jnp.float32)


def pick_kernel(places, own_plan_ref, other_plan_ref, *refs):
    piece_refs = refs[: len(places)]
    own_hbm, other_hbm, own_ref, other_ref, wave_ref, piece_sems, own_sems, other_sems = refs[
        len(places) :
    ]
    op = lax.axis_index("op")
    copies = []
    for i, (base, step) in enumerate(places):
        piece = lax.rem(op // CORES - step + Z, Z)
        copies.append(
            pltpu.make_async_copy(
                piece_refs[i],
                wave_ref.at[pl.ds(base, piece_refs[i].shape[0]), piece],
                piece_sems.at[i],
            )
        )
    for copy in copies:
        copy.start()
    for copy in copies:
        copy.wait()
    halves = (
        (own_plan_ref, own_ref, own_hbm, own_sems),
        (other_plan_ref, other_ref, other_hbm, other_sems),
    )
    for plan_ref, picked_ref, picked_hbm, sems in halves:

        def pick(step, carry):
            for i in range(UNROLL):
                n = step * UNROLL + i
                picked_ref[n] = wave_ref[(plan_ref[n] >> GROUP_BITS) & (2**SECTOR_BITS - 1)]
            rows = pl.ds(step * UNROLL, UNROLL)
            pltpu.make_async_copy(picked_ref.at[rows], picked_hbm.at[rows], sems.at[step]).start()
            return carry

        lax.fori_loop(0, plan_ref[PLAN - 1], pick, 0)
    for plan_ref, picked_ref, picked_hbm, sems in halves:

        def finish(step, carry):
            rows = pl.ds(step * UNROLL, UNROLL)
            pltpu.make_async_copy(picked_ref.at[rows], picked_hbm.at[rows], sems.at[step]).wait()
            return carry

        lax.fori_loop(0, plan_ref[PLAN - 1], finish, 0)


def own_kernel(
    plan_ref,
    arrived_hbm,
    left_hbm,
    picked_hbm,
    sums_ref,
    arrived_ref,
    left_ref,
    grouped_ref,
    sems,
    picked_ref,
    more_sems,
):
    steps = plan_ref[PLAN - 1]

    def picked_copy(step):
        rows = pl.ds(step * UNROLL, UNROLL)
        return pltpu.make_async_copy(picked_hbm.at[rows], picked_ref.at[rows], more_sems.at[step])

    def start_step(step, carry):
        picked_copy(step).start()
        return carry

    def start_more():
        lax.fori_loop(0, steps, start_step, 0)

    def wait_step(step):
        picked_copy(step).wait()

    half_products(
        plan_ref,
        arrived_hbm,
        left_hbm,
        lambda n, sector: picked_ref[n],
        arrived_ref,
        left_ref,
        grouped_ref,
        sems,
        lambda: None,
        wait_step,
        start_more,
    )

    def left(pair, carry):
        for j in range(2):
            sums_ref[pair * 2 + j] = left_sum(left_ref, grouped_ref, pair * 2 + j)
        return carry

    lax.fori_loop(0, 4, left, 0)


def other_kernel(
    plan_ref,
    arrived_hbm,
    left_hbm,
    picked_hbm,
    sums_hbm,
    out_ref,
    arrived_ref,
    left_ref,
    grouped_ref,
    sems,
    picked_ref,
    sums_ref,
    more_sems,
):
    sums_copy = pltpu.make_async_copy(sums_hbm, sums_ref, more_sems.at[PICKED // UNROLL])
    steps = plan_ref[PLAN - 1]

    def picked_copy(step):
        rows = pl.ds(step * UNROLL, UNROLL)
        return pltpu.make_async_copy(picked_hbm.at[rows], picked_ref.at[rows], more_sems.at[step])

    def start_step(step, carry):
        picked_copy(step).start()
        return carry

    def start_more():
        lax.fori_loop(0, steps, start_step, 0)
        sums_copy.start()

    def wait_step(step):
        picked_copy(step).wait()

    half_products(
        plan_ref,
        arrived_hbm,
        left_hbm,
        lambda n, sector: picked_ref[n],
        arrived_ref,
        left_ref,
        grouped_ref,
        sems,
        lambda: None,
        wait_step,
        start_more,
    )
    sums_copy.wait()
    width = sums_ref.shape[2]

    def left(pair, carry):
        both = []
        for j in range(2):
            t = pair * 2 + j
            total = sums_ref[t] + left_sum(left_ref, grouped_ref, t)
            both.append(total.reshape(16, 8, width))
        rows = jnp.stack(both, axis=1).reshape(16, 16, width)
        out_ref[:, pl.ds(pl.multiple_of(pair * 16, 16), 16), :] = rows.astype(out_ref.dtype)
        return carry

    lax.fori_loop(0, 4, left, 0)


SMEM = pl.BlockSpec(memory_space=pltpu.SMEM)
VMEM = pl.BlockSpec(memory_space=pltpu.VMEM)
HBM = pl.BlockSpec(memory_space=pl.ANY)


def work_space(arrived, left):
    slots, width, _ = arrived.shape
    terms = left.shape[0]
    return [
        pltpu.VMEM((slots, width, width), jnp.bfloat16),
        pltpu.VMEM((terms, width, width), jnp.bfloat16),
        pltpu.VMEM((terms + 1, width, width), jnp.float32),
        pltpu.SemaphoreType.DMA((2,)),
    ]


COST = pl.CostEstimate(flops=2 * 128 * 128**3, bytes_accessed=16 * 2**20, transcendentals=0)


def pick_blocks(own_plan, other_plan, pieces):
    width = pieces[0][0].shape[2]
    count = len(pieces)
    block = (PICKED, Z, 16, width)
    return pl.pallas_call(
        functools.partial(pick_kernel, [p[1:] for p in pieces]),
        out_shape=(jax.ShapeDtypeStruct(block, jnp.bfloat16),) * 2,
        in_specs=[SMEM, SMEM] + [HBM] * count,
        out_specs=(HBM, HBM),
        scratch_shapes=[
            pltpu.VMEM(block, jnp.bfloat16),
            pltpu.VMEM(block, jnp.bfloat16),
            pltpu.VMEM((X * Y * 8, Z, 16, width), jnp.bfloat16),
            pltpu.SemaphoreType.DMA((count,)),
            pltpu.SemaphoreType.DMA((PICKED // UNROLL,)),
            pltpu.SemaphoreType.DMA((PICKED // UNROLL,)),
        ],
        compiler_params=pltpu.CompilerParams(vmem_limit_bytes=60 * 2**20),
        cost_estimate=COST,
        name="pick_blocks",
    )(own_plan, other_plan, *[p[0] for p in pieces])


def own_products(plan, arrived, left, picked):
    width = arrived.shape[1]
    return pl.pallas_call(
        own_kernel,
        out_shape=jax.ShapeDtypeStruct((8, width, width), jnp.float32),
        in_specs=[SMEM, HBM, HBM, HBM],
        out_specs=VMEM,
        scratch_shapes=work_space(arrived, left)
        + [
            pltpu.VMEM(picked.shape, picked.dtype),
            pltpu.SemaphoreType.DMA((PICKED // UNROLL,)),
        ],
        compiler_params=pltpu.CompilerParams(vmem_limit_bytes=60 * 2**20),
        cost_estimate=COST,
        name="own_products",
    )(plan, arrived, left, picked)


def other_products(plan, arrived, left, picked, sums):
    width = arrived.shape[1]
    return pl.pallas_call(
        other_kernel,
        out_shape=jax.ShapeDtypeStruct((16, 64, width), jnp.bfloat16),
        in_specs=[SMEM, HBM, HBM, HBM, HBM],
        out_specs=VMEM,
        scratch_shapes=work_space(arrived, left)
        + [
            pltpu.VMEM(picked.shape, picked.dtype),
            pltpu.VMEM(sums.shape, sums.dtype),
            pltpu.SemaphoreType.DMA((PICKED // UNROLL + 1,)),
        ],
        compiler_params=pltpu.CompilerParams(vmem_limit_bytes=60 * 2**20),
        cost_estimate=COST,
        name="other_products",
    )(plan, arrived, left, picked, sums)


def spread_column(wavefunction, targets):
    op = lax.axis_index("op")
    _, sectors, rows, cols = wavefunction.shape
    piece = lax.dynamic_slice(
        wavefunction, (op % CORES, 0, (op // CORES) * 16, 0), (1, sectors, 16, cols)
    )
    marks = jnp.pad(targets.astype(jnp.bfloat16), ((0, 16 - sectors), (0, cols - targets.shape[1])))
    load = jnp.concatenate([piece, marks[None, None]], axis=1)
    columns = [[x * Y + y for y in range(Y)] for x in range(X)]
    return lax.all_to_all(
        jnp.broadcast_to(load, (Y,) + load.shape[1:]),
        "sector",
        split_axis=0,
        concat_axis=0,
        axis_index_groups=columns,
        tiled=True,
    )


def per_device(wavefunction, right_blocks, left_blocks, targets):
    sectors, terms, width, _ = right_blocks.shape
    pairs = sectors * terms
    groups = lax.axis_size("sector")
    swap = functools.partial(lax.ppermute, axis_name="op", perm=core_swap())
    ring_up = functools.partial(lax.ppermute, axis_name="op", perm=z_shift(1))
    ring_down = functools.partial(lax.ppermute, axis_name="op", perm=z_shift(-1))
    tie = lax.optimization_barrier
    packed = pack(targets, right_blocks, groups)
    column = spread_column(wavefunction, targets)
    columns = [column] + [lax.ppermute(column, "sector", x_shift(d)) for d in range(1, X)]
    packed, *_ = tie((packed, *columns))
    arrived = lax.all_to_all(packed, "sector", split_axis=0, concat_axis=0, tiled=True)
    own_left = left_blocks.reshape(pairs, width, width)

    size = Y * sectors
    own_plan = make_plan([c[:, sectors] for c in columns])
    blocks = [c[:, :sectors].reshape(size, 16, width) for c in columns]
    starts = [jnp.concatenate(blocks[:2]), jnp.concatenate(blocks[2:])]
    ups = [[s] for s in starts]
    downs = [[s] for s in starts]
    for step in range(1, Z // 2):
        for chain in ups:
            chain.append(ring_up(chain[-1]))
        for chain in downs:
            chain.append(ring_down(chain[-1]))
        if step == 2:
            ups[1][2], own_left = tie((ups[1][2], own_left))
            other_left = swap(own_left)
        if step == 3:
            ups[0][3], other_plan = tie((ups[0][3], swap(own_plan)))
    pieces = []
    last = []
    for n, start in enumerate(starts):
        base = 2 * size * n
        pieces.append((start, base, 0))
        for step in range(1, Z // 2):
            pieces.append((ups[n][step], base, step))
            pieces.append((downs[n][step], base, -step))
        last.append((ring_up(ups[n][-1][:size]), base, Z // 2))
        last.append((ring_down(downs[n][-1][size:]), base + size, Z // 2))
    pieces += last

    own_picked, picked = pick_blocks(own_plan, other_plan, pieces)
    arrived, own_picked, picked = tie((arrived, own_picked, picked))
    other_arrived = swap(arrived)
    sums = own_products(own_plan, arrived, own_left, own_picked)
    partial_value = other_products(other_plan, other_arrived, other_left, picked, sums)
    got = lax.all_to_all(partial_value, "op", split_axis=0, concat_axis=0, tiled=True)
    return jnp.sum(got.reshape(Z, CORES, 8, 8, width).astype(jnp.float32), axis=0)


def solution(mesh):
    return jax.shard_map(
        per_device,
        mesh=mesh,
        in_specs=(
            P(None, "sector", None, None),
            P("sector", "op", None, None),
            P("sector", "op", None, None),
            P("sector", "op"),
        ),
        out_specs=P(None, "sector", "op", None),
        check_vma=False,
    )
```
